32 devices in a mesh: group: 8 (over z, core), inner: 4 (over y, x).
Axes of the slice: x: 2, y: 2, z: 4, core: 2. Of those that a mesh axis runs over, the one named last changes fastest.
Arguments:
- embeddings: bfloat16 [16384, 256], P(('group', 'inner')), may hold values from -6 to 6
- cluster_id: int32 [16384], P(('group', 'inner')), may hold values from 0 to 511, as said below
- order_rank: int32 [16384], P(('group', 'inner')), may hold values from 0 to 16383, each once
- send_slot: int32 [16384], P(('group', 'inner')), may hold values from 0 to 1023, as said below
- usable: int32 [16384], P(('group', 'inner')), may hold values 0 or 1
Outputs:
- best_cosine: float32 [16384], P(('group', 'inner'))
The draws below stay inside these ranges and needn't reach their ends.
Inputs may be any that keep to these rules, and one draw needn't show every extreme that they name: send_slot // 128 is the group that owns a row and send_slot % 128 its slot among the 128 slots from its device to that group; no two rows of one device share a value. For each group and each index of inner, the rows sent to that group by the 8 devices with that inner index number at most 768, and some such count equals 768 in every draw; half of the devices fill all 128 slots to some group. A row owned by group g has a cluster id from g * 64 to (g + 1) * 64 - 1. Among the rows sent to one group by the devices of one inner index, at most 192 have any one value of cluster_id % 4, and that count is reached in every draw.
All inputs are finite; a program needn't handle non-finite values. No bound on the sum of `usable` on one device may be relied on, other than what follows from the above.
Results may differ from the reference program's by a relative error of at most 0.0016.
Values may be sent and summed in bfloat16 or wider, within the bound.
A program may use at most 64 MiB of HBM per device.

```python
import math
import jax
import jax.numpy as jnp
from jax import lax

D = 256
ROWS_DEV = 512
CLUST_GRP = 64
ROWS = 16384
N_GROUP = 8
N_INNER = 4


def slot_plan(key):
    groups = N_GROUP
    inner = N_INNER
    devices = groups * inner
    share = ROWS_DEV // groups
    capacity = 2 * share
    heavy_key, kind_key, place_key, order_key = jax.random.split(key, 4)
    heavy = jax.random.permutation(heavy_key, groups) < groups // 2

    def half_groups(subkey):
        return jax.random.permutation(subkey, groups) < groups // 2

    def slot_order(subkey):
        return jax.random.permutation(subkey, capacity)

    def row_order(subkey):
        return jax.random.permutation(subkey, ROWS_DEV)
    kinds = jax.vmap(half_groups)(jax.random.split(kind_key, inner))
    loaded = jnp.transpose(kinds).reshape(devices)
    counts = jnp.where(loaded[:, None], jnp.where(heavy[None, :], capacity, 0), share).astype(jnp.int32)
    orders = jax.vmap(slot_order)(jax.random.split(place_key, devices * groups)).reshape(devices, groups, capacity)
    used = (orders < counts[:, :, None]).reshape(devices, groups * capacity)
    listed = jnp.argsort(1 - used.astype(jnp.int32), axis=1, stable=True)[:, :ROWS_DEV]
    shuffle = jax.vmap(row_order)(jax.random.split(order_key, devices))
    chosen = jnp.take_along_axis(listed, shuffle, axis=1)
    return chosen.reshape(devices * ROWS_DEV).astype(jnp.int32)


def draw_send_slot(key, part):
    planned = slot_plan(key)
    return planned


def draw_cluster_id(key, part):
    planned = slot_plan(key)
    key = jax.random.fold_in(key, 5)
    capacity = 2 * ROWS_DEV // N_GROUP
    total_rows = N_GROUP * N_INNER * ROWS_DEV
    source = jnp.arange(total_rows, dtype=jnp.int32) // ROWS_DEV
    owner = planned // capacity
    arrival_device = owner * N_INNER + source % N_INNER
    arrival_spot = source // N_INNER * capacity + planned % capacity
    sort_value = (arrival_device * (N_GROUP * capacity) + arrival_spot).astype(jnp.int32)
    ordering = jnp.argsort(sort_value, stable=True)
    sorted_device = arrival_device[ordering]
    first_index = jnp.searchsorted(sorted_device, sorted_device, side='left').astype(jnp.int32)
    sorted_rank = jnp.arange(total_rows, dtype=jnp.int32) - first_index
    arrival_rank = jnp.zeros((total_rows,), jnp.int32).at[ordering].set(sorted_rank)
    residue = (arrival_rank + arrival_device) % N_INNER
    upper = jax.random.randint(key, (total_rows,), 0, CLUST_GRP // N_INNER, dtype=jnp.int32)
    member = residue + N_INNER * upper
    return (owner * CLUST_GRP + member).astype(jnp.int32)


def with_ends(result, key, smallest, largest):
    longest = result.shape.index(max(result.shape))
    spots = []
    for shift in (0, 1):
        where = [jax.random.randint(jax.random.fold_in(key, axis), (), 0, length) for axis, length in enumerate(result.shape)]
        where[longest] = (where[longest] + shift) % result.shape[longest]
        spots.append(tuple(where))
    return result.at[spots[0]].set(smallest).at[spots[1]].set(largest)


def levels(rng, extent, pieces, least, largest):
    factor_of = 1.0
    for dim, parts in pieces:
        draws = jax.random.uniform(jax.random.fold_in(jax.random.fold_in(rng, 6), dim), (parts,), jnp.float32, least / len(pieces), largest / len(pieces))
        factor_of = factor_of * jnp.repeat(jnp.exp(draws), extent[dim] // parts).reshape((-1,) + (1,) * (len(extent) - 1 - dim))
    return factor_of


def noise(own_key, dims, width, reach, pieces=(), held_as=jnp.bfloat16):
    result = width * jax.random.normal(own_key, dims, jnp.float32)
    if pieces:
        result = result * levels(own_key, dims, pieces, -0.22, 0.18)
    return jnp.clip(result, -reach, reach).astype(held_as)


def setup_inputs(seed: int = 0) -> dict:
    splits = jax.random.split(jax.random.key(seed), 6)
    return {
        "embeddings": noise(splits[0], (ROWS, D), 1.0, 6.0, ((0, 32),)),
        "cluster_id": draw_cluster_id(jax.random.fold_in(splits[5], 71), 0),
        "order_rank": jax.random.permutation(splits[2], ROWS).astype(jnp.int32),
        "send_slot": draw_send_slot(jax.random.fold_in(splits[5], 71), 0),
        "usable": with_ends((jax.random.randint(splits[4], (ROWS,), 0, 8) < 7).astype(jnp.int32), jax.random.fold_in(splits[4], 1), 0, 1),
    }


def unit_rows(embeddings):
    values = embeddings.astype(jnp.float32)
    inverse = lax.rsqrt(lax.optimization_barrier(jnp.sum(values * values, axis=1, keepdims=True)) + 1e-06)
    return (values * inverse).astype(jnp.bfloat16)

def reference(embeddings, cluster_id, order_rank, send_slot, usable):
    capacity = 2 * ROWS_DEV // N_GROUP
    total_rows = embeddings.shape[0]
    normed = unit_rows(embeddings)
    source = jnp.arange(total_rows, dtype=jnp.int32) // ROWS_DEV
    target = send_slot // capacity
    group_span = N_GROUP * N_INNER * capacity
    placement = (target * group_span + source * capacity + send_slot % capacity).astype(jnp.int32)
    total_slots = N_GROUP * group_span
    slot_rows = jnp.zeros((total_slots, D), jnp.bfloat16).at[placement].set(normed)
    query_cluster = jnp.full((total_slots,), -1, jnp.int32).at[placement].set(cluster_id)
    member_cluster = jnp.where(usable > 0, cluster_id, -1).astype(jnp.int32)
    key_cluster = jnp.full((total_slots,), -1, jnp.int32).at[placement].set(member_cluster)
    slot_rank = jnp.zeros((total_slots,), jnp.int32).at[placement].set(order_rank)
    height = math.gcd(group_span, 1024)
    per_group = group_span // height

    def score_block(block_index):
        group_start = block_index // per_group * group_span
        query_start = group_start + block_index % per_group * height
        queries = lax.dynamic_slice_in_dim(slot_rows, query_start, height, 0)
        group_rows = lax.dynamic_slice_in_dim(slot_rows, group_start, group_span, 0)
        query_tags = lax.dynamic_slice_in_dim(query_cluster, query_start, height, 0)
        query_order = lax.dynamic_slice_in_dim(slot_rank, query_start, height, 0)
        key_tags = lax.dynamic_slice_in_dim(key_cluster, group_start, group_span, 0)
        key_order = lax.dynamic_slice_in_dim(slot_rank, group_start, group_span, 0)
        scores = jnp.dot(queries, group_rows.T, preferred_element_type=jnp.float32)
        matched = (query_tags[:, None] == key_tags[None, :]) & (key_order[None, :] < query_order[:, None])
        return lax.optimization_barrier(jnp.max(jnp.where(matched, scores, -1.0), axis=1))
    results = lax.map(score_block, jnp.arange(N_GROUP * per_group, dtype=jnp.int32))
    return results.reshape(-1)[placement]
```

```python
import functools

import jax
import jax.numpy as jnp
from jax import lax
from jax.experimental import pallas as pl
from jax.experimental.pallas import tpu as pltpu
from jax.sharding import PartitionSpec as P

MESH = pl.DeviceIdType.MESH
BASE = 64
HALF = 128
TAGS = 16


def round_up(value, step):
    return (value + step - 1) // step * step


def partner(me, k):
    result, bit = me, 1
    while bit <= k:
        if k & bit:
            result = result + bit * (1 - 2 * lax.rem(lax.div(me, bit), 2))
        bit *= 2
    return result


def split_rows(value):
    high = value.astype(jnp.bfloat16).astype(jnp.float32)
    rest = value - high
    mid = rest.astype(jnp.bfloat16).astype(jnp.float32)
    low = rest - mid
    row = lax.broadcasted_iota(jnp.int32, (TAGS, value.shape[1]), 0)
    parts = jnp.where(row == 0, high, jnp.where(row == 1, mid, jnp.where(row == 2, low, 0.0)))
    return parts.astype(jnp.bfloat16)


def join_rows(parts):
    return (parts[0:1] + parts[1:2]) + parts[2:3]


def one_hot(position, rows):
    row = lax.broadcasted_iota(jnp.int32, (rows, position.shape[1]), 0)
    return jnp.where(row == position, 1.0, 0.0).astype(jnp.bfloat16)


def dot_nt(a, b):
    return lax.dot_general(a, b, (((1,), (1,)), ((), ())), preferred_element_type=jnp.float32)


def dot_nn(a, b):
    return jnp.dot(a, b, preferred_element_type=jnp.float32)


def kernel(
    groups, inner, capacity, lanes, bin_rows, bin_lanes,
    emb_ref, cid_ref, rank_ref, slot_ref, use_ref, out_ref,
    place, pick, limit,
    tag_out, tag_in, row_out, row_in, tag2_out, tag2_in, row2_out, row2_in,
    best_out, best_in, back_out, back_in,
    tag_s, tag_r, row_s, row_r, tag2_s, tag2_r, row2_s, row2_r, best_s, best_r, back_s, back_r,
):
    rows, width = emb_ref.shape
    halves = width // HALF
    total = inner * bin_rows
    my_group, my_inner = lax.axis_index("group"), lax.axis_index("inner")
    group_of = [partner(my_group, k) for k in range(groups)]
    inner_of = [partner(my_inner, k) for k in range(inner)]

    barrier = pltpu.get_barrier_semaphore()
    for k in range(1, groups):
        pl.semaphore_signal(barrier, inc=1, device_id={"group": group_of[k]}, device_id_type=MESH)
    for k in range(1, inner):
        pl.semaphore_signal(barrier, inc=1, device_id={"inner": inner_of[k]}, device_id_type=MESH)

    def remote(src, dst, send, recv, axis, peer):
        return pltpu.make_async_remote_copy(
            src_ref=src, dst_ref=dst, send_sem=send, recv_sem=recv,
            device_id={axis: peer}, device_id_type=MESH,
        )

    order = list(range(groups - 2, 0, -2))
    order = [k for pair in order for k in (pair, pair + 1)] + [1]
    inner_order = list(range(inner - 1, 0, -1))
    tag_copy = {k: remote(tag_out.at[k], tag_in.at[k], tag_s.at[k], tag_r.at[k], "group", group_of[k]) for k in order}
    row_copy = {
        (h, k): remote(row_out.at[h, k], row_in.at[h, k], row_s.at[h, k], row_r.at[h, k], "group", group_of[k])
        for h in range(halves) for k in order
    }
    tag2_copy = {k: remote(tag2_out.at[k], tag2_in.at[k], tag2_s.at[k], tag2_r.at[k], "inner", inner_of[k]) for k in inner_order}
    row2_copy = {
        (h, k): remote(row2_out.at[h, k], row2_in.at[h, k], row2_s.at[h, k], row2_r.at[h, k], "inner", inner_of[k])
        for h in range(halves) for k in inner_order
    }
    best_copy = {k: remote(best_out.at[k], best_in.at[k], best_s.at[k], best_r.at[k], "inner", inner_of[k]) for k in inner_order}
    back_copy = {k: remote(back_out.at[k], back_in.at[k], back_s.at[k], back_r.at[k], "group", group_of[k]) for k in order}

    cluster = cid_ref[...]
    rank = rank_ref[...]
    slot = slot_ref[...]
    row = lax.broadcasted_iota(jnp.int32, (TAGS, rows), 0)
    tags = jnp.where(row == 0, jnp.bitwise_and(cluster, BASE - 1), 0)
    tags = jnp.where(row == 1, 1, tags)
    tags = jnp.where(row == 2, use_ref[...], tags)
    tags = jnp.where(row == 3, jnp.bitwise_and(rank, BASE - 1), tags)
    tags = jnp.where(row == 4, jnp.bitwise_and(jnp.right_shift(rank, 6), BASE - 1), tags)
    tags = jnp.where(row == 5, jnp.right_shift(rank, 12), tags)
    tags = tags.astype(jnp.float32).astype(jnp.bfloat16)

    for k in order + [0]:
        wanted = slot - group_of[k] * capacity
        if capacity < lanes:
            wanted = jnp.where(wanted < capacity, wanted, -1)
        hot = one_hot(wanted, lanes)
        place[k] = hot
        block = dot_nt(tags, hot).astype(jnp.bfloat16)
        if k:
            tag_out[k] = block
        else:
            tag_in[0] = block

    pl.semaphore_wait(barrier, groups + inner - 2)
    for k in order:
        tag_copy[k].start()

    values = emb_ref[...].astype(jnp.float32)
    inverse = lax.rsqrt(jnp.sum(values * values, axis=1, keepdims=True) + 1e-06)
    unit = (values * inverse).astype(jnp.bfloat16)
    for k in order + [0]:
        block = dot_nn(place[k], unit).astype(jnp.bfloat16)
        for h in range(halves):
            part = block[:, h * HALF:(h + 1) * HALF]
            if k:
                row_out[h, k] = part
            else:
                row_in[h, 0] = part
        if k:
            row_copy[0, k].start()
    for h in range(1, halves):
        for k in order:
            row_copy[h, k].start()

    before = jnp.where(
        lax.broadcasted_iota(jnp.int32, (lanes, lanes), 0) < lax.broadcasted_iota(jnp.int32, (lanes, lanes), 1),
        1.0, 0.0,
    ).astype(jnp.bfloat16)
    bin_pad = round_up(inner, TAGS)
    seen = jnp.zeros((bin_pad, 1), jnp.float32)
    for k in order:
        tag_copy[k].wait_recv()
    for k in range(groups):
        arrived = tag_in[k].astype(jnp.float32)
        residue = jnp.bitwise_and(arrived[0:1].astype(jnp.int32), inner - 1)
        filled = arrived[1:2] > 0.5
        relative = jnp.full_like(residue, -1)
        for j in range(inner):
            relative = jnp.where(filled & (residue == inner_of[j]), j, relative)
        member = one_hot(relative, bin_pad)
        member_f = member.astype(jnp.float32)
        spot = dot_nn(member, before) + seen
        seen = seen + jnp.sum(member_f, axis=1, keepdims=True)
        spot = jnp.sum(member_f * spot, axis=0, keepdims=True).astype(jnp.int32)
        goal = jnp.where(filled, relative * bin_rows + spot, -1)
        pick[:, k * lanes:(k + 1) * lanes] = one_hot(goal, total)
    arrived_tags = jnp.concatenate([tag_in[k] for k in range(groups)], axis=1)
    for k in inner_order + [0]:
        block = dot_nt(arrived_tags, pick[k * bin_rows:(k + 1) * bin_rows, :]).astype(jnp.bfloat16)
        if bin_rows < bin_lanes:
            block = jnp.concatenate([block, jnp.zeros((TAGS, bin_lanes - bin_rows), jnp.bfloat16)], axis=1)
        if k:
            tag2_out[k] = block
            tag2_copy[k].start()
        else:
            tag2_in[0] = block

    def forward(h):
        for k in order:
            row_copy[h, k].wait_recv()
        arrived_rows = row_in[h].reshape(groups * lanes, HALF)
        for k in inner_order + [0]:
            block = dot_nn(pick[k * bin_rows:(k + 1) * bin_rows, :], arrived_rows).astype(jnp.bfloat16)
            if k:
                row2_out[h, k] = block
                row2_copy[h, k].start()
            else:
                row2_in[h, 0] = block

    for h in range(halves - 1):
        forward(h)

    for k in inner_order:
        tag2_copy[k].wait_recv()
    same = lax.broadcasted_iota(jnp.int32, (bin_lanes, bin_lanes), 0) == lax.broadcasted_iota(
        jnp.int32, (bin_lanes, bin_lanes), 1
    )
    eye = jnp.where(same, 1.0, 0.0).astype(jnp.bfloat16)
    key_cluster, key_rank = [], []
    for k in range(inner):
        columns = dot_nt(eye, tag2_in[k])[:bin_rows]
        key_cluster.append(jnp.where(columns[:, 1:2] * columns[:, 2:3] > 0.5, columns[:, 0:1], -1.0))
        key_rank.append(columns[:, 3:4] + BASE * columns[:, 4:5] + (BASE * BASE) * columns[:, 5:6])
    for q in range(inner):
        lines = tag2_in[q].astype(jnp.float32)[:, :bin_rows]
        query_cluster = lines[0:1]
        query_rank = lines[3:4] + BASE * lines[4:5] + (BASE * BASE) * lines[5:6]
        for k in range(inner):
            matched = (key_cluster[k] == query_cluster) & (key_rank[k] < query_rank)
            limit[q, k * bin_rows:(k + 1) * bin_rows, :] = jnp.where(matched, 1e30, -1.0)

    forward(halves - 1)

    for h in range(halves):
        for k in inner_order:
            row2_copy[h, k].wait_recv()
    keys = jnp.concatenate([row2_in[h].reshape(total, HALF) for h in range(halves)], axis=1)
    for q in inner_order + [0]:
        queries = jnp.concatenate([row2_in[h, q] for h in range(halves)], axis=1)
        scores = jnp.minimum(dot_nt(keys, queries), limit[q])
        best = jnp.maximum(jnp.max(scores, axis=0, keepdims=True), -1.0)
        if bin_rows < bin_lanes:
            best = jnp.concatenate([best, jnp.zeros((1, bin_lanes - bin_rows), jnp.float32)], axis=1)
        best = jnp.broadcast_to(best, (8, bin_lanes))
        if q:
            best_out[q] = best
            best_copy[q].start()
        else:
            best_in[0] = best

    for k in inner_order:
        best_copy[k].wait_recv()
    spread = jnp.zeros((TAGS, groups * lanes), jnp.float32)
    for k in range(inner):
        parts = split_rows(best_in[k, 0:1, :])[:, :bin_rows]
        spread = spread + dot_nn(parts, pick[k * bin_rows:(k + 1) * bin_rows, :])
    spread = join_rows(spread)
    for k in order + [0]:
        block = jnp.broadcast_to(spread[:, k * lanes:(k + 1) * lanes], (8, lanes))
        if k:
            back_out[k] = block
            back_copy[k].start()
        else:
            back_in[0] = block

    for k in order:
        back_copy[k].wait_recv()
    parts = jnp.concatenate([split_rows(back_in[k, 0:1, :]) for k in range(groups)], axis=1)
    result = dot_nn(parts, place[...].reshape(groups * lanes, rows))
    out_ref[...] = join_rows(result)

    for copies in (tag_copy, row_copy, tag2_copy, row2_copy, best_copy, back_copy):
        for copy in copies.values():
            copy.wait_send()


def local(embeddings, cluster_id, order_rank, send_slot, usable):
    groups, inner = lax.axis_size("group"), lax.axis_size("inner")
    rows, width = embeddings.shape
    capacity = 2 * rows // groups
    lanes = round_up(capacity, 128)
    bin_rows = 3 * rows // 2 // inner
    bin_lanes = round_up(bin_rows, 128)
    halves = width // HALF
    total = inner * bin_rows
    bf16, f32 = jnp.bfloat16, jnp.float32
    dma = pltpu.SemaphoreType.DMA
    sems = []
    for shape in ((groups,), (halves, groups), (inner,), (halves, inner), (inner,), (groups,)):
        sems += [dma(shape), dma(shape)]
    out = pl.pallas_call(
        functools.partial(kernel, groups, inner, capacity, lanes, bin_rows, bin_lanes),
        out_shape=jax.ShapeDtypeStruct((1, rows), f32),
        in_specs=[pl.BlockSpec(memory_space=pltpu.VMEM)] * 5,
        out_specs=pl.BlockSpec(memory_space=pltpu.VMEM),
        scratch_shapes=[
            pltpu.VMEM((groups, lanes, rows), bf16),
            pltpu.VMEM((total, groups * lanes), bf16),
            pltpu.VMEM((inner, total, bin_rows), f32),
            pltpu.VMEM((groups, TAGS, lanes), bf16),
            pltpu.VMEM((groups, TAGS, lanes), bf16),
            pltpu.VMEM((halves, groups, lanes, HALF), bf16),
            pltpu.VMEM((halves, groups, lanes, HALF), bf16),
            pltpu.VMEM((inner, TAGS, bin_lanes), bf16),
            pltpu.VMEM((inner, TAGS, bin_lanes), bf16),
            pltpu.VMEM((halves, inner, bin_rows, HALF), bf16),
            pltpu.VMEM((halves, inner, bin_rows, HALF), bf16),
            pltpu.VMEM((inner, 8, bin_lanes), f32),
            pltpu.VMEM((inner, 8, bin_lanes), f32),
            pltpu.VMEM((groups, 8, lanes), f32),
            pltpu.VMEM((groups, 8, lanes), f32),
        ] + sems,
        compiler_params=pltpu.CompilerParams(
            collective_id=0, has_side_effects=True, vmem_limit_bytes=40 * 1024 * 1024
        ),
        name="dedup",
    )(
        embeddings,
        cluster_id.reshape(1, rows),
        order_rank.reshape(1, rows),
        send_slot.reshape(1, rows),
        usable.reshape(1, rows),
    )
    return out.reshape(rows)


def solution(mesh):
    placed = (
        P(("group", "inner"), None),
        P(("group", "inner")),
        P(("group", "inner")),
        P(("group", "inner")),
        P(("group", "inner")),
    )
    return jax.shard_map(
        local, mesh=mesh, in_specs=placed, out_specs=P(("group", "inner")), check_vma=False
    )
```

```python
import functools

import jax
import jax.numpy as jnp
from jax import lax
from jax.experimental import pallas as pl
from jax.experimental.pallas import tpu as pltpu
from jax.sharding import PartitionSpec as P

MESH = pl.DeviceIdType.MESH
BASE = 64
HALF = 128
TAGS = 16


def round_up(value, step):
    return (value + step - 1) // step * step


def partner(me, k):
    result, bit = me, 1
    while bit <= k:
        if k & bit:
            result = result + bit * (1 - 2 * lax.rem(lax.div(me, bit), 2))
        bit *= 2
    return result


def split_rows(value):
    high = value.astype(jnp.bfloat16).astype(jnp.float32)
    rest = value - high
    mid = rest.astype(jnp.bfloat16).astype(jnp.float32)
    low = rest - mid
    row = lax.broadcasted_iota(jnp.int32, (TAGS, value.shape[1]), 0)
    parts = jnp.where(row == 0, high, jnp.where(row == 1, mid, jnp.where(row == 2, low, 0.0)))
    return parts.astype(jnp.bfloat16)


def join_rows(parts):
    return (parts[0:1] + parts[1:2]) + parts[2:3]


def one_hot(position, rows):
    row = lax.broadcasted_iota(jnp.int32, (rows, position.shape[1]), 0)
    return jnp.where(row == position, 1.0, 0.0).astype(jnp.bfloat16)


def dot_nt(a, b):
    return lax.dot_general(a, b, (((1,), (1,)), ((), ())), preferred_element_type=jnp.float32)


def dot_nn(a, b):
    return jnp.dot(a, b, preferred_element_type=jnp.float32)


def kernel(
    groups, inner, capacity, lanes, bin_rows, bin_lanes,
    emb_hbm, cid_hbm, rank_hbm, slot_hbm, use_hbm, out_ref,
    emb_ref, cid_ref, rank_ref, slot_ref, use_ref, load,
    place, pick, limit,
    tag_out, tag_in, row_out, row_in, tag2_out, tag2_in, row2_out, row2_in,
    back_place, back_out, back_in,
    tag_s, tag_r, row_s, row_r, tag2_s, tag2_r, row2_s, row2_r, back_s, back_r,
):
    rows, width = emb_ref.shape
    halves = width // HALF
    total = inner * bin_rows
    my_group, my_inner = lax.axis_index("group"), lax.axis_index("inner")
    group_of = [partner(my_group, k) for k in range(groups)]
    inner_of = [partner(my_inner, k) for k in range(inner)]

    order = list(range(groups - 2, 0, -2))
    order = [k for pair in order for k in (pair, pair + 1)] + [1]
    inner_order = list(range(inner - 1, 0, -1))
    barrier = pltpu.get_barrier_semaphore()
    for k in order:
        pl.semaphore_signal(barrier, inc=1, device_id={"group": group_of[k]}, device_id_type=MESH)
    for k in inner_order:
        pl.semaphore_signal(barrier, inc=1, device_id={"inner": inner_of[k]}, device_id_type=MESH)

    slot_load, emb_load, cid_load, rank_load, use_load = [
        pltpu.make_async_copy(src, dst, load.at[n])
        for n, (src, dst) in enumerate(
            ((slot_hbm, slot_ref), (emb_hbm, emb_ref), (cid_hbm, cid_ref), (rank_hbm, rank_ref), (use_hbm, use_ref))
        )
    ]
    for copy in (slot_load, emb_load, cid_load, rank_load, use_load):
        copy.start()


    def remote(src, dst, send, recv, axis, peer):
        return pltpu.make_async_remote_copy(
            src_ref=src, dst_ref=dst, send_sem=send, recv_sem=recv,
            device_id={axis: peer}, device_id_type=MESH,
        )

    tag_copy = {k: remote(tag_out.at[k], tag_in.at[k], tag_s.at[k], tag_r.at[k], "group", group_of[k]) for k in order}
    row_copy = {
        (h, k): remote(row_out.at[h, k], row_in.at[h, k], row_s.at[h, k], row_r.at[h, k], "group", group_of[k])
        for h in range(halves) for k in order
    }
    tag2_copy = {k: remote(tag2_out.at[k], tag2_in.at[k], tag2_s.at[k], tag2_r.at[k], "inner", inner_of[k]) for k in inner_order}
    row2_copy = {
        (h, k): remote(row2_out.at[h, k], row2_in.at[h, k], row2_s.at[h, k], row2_r.at[h, k], "inner", inner_of[k])
        for h in range(halves) for k in inner_order
    }
    back_copy = {
        (j, k): pltpu.make_async_remote_copy(
            src_ref=back_out.at[j, k], dst_ref=back_in.at[j, k], send_sem=back_s.at[j, k], recv_sem=back_r.at[j, k],
            device_id=(group_of[k], inner_of[j]), device_id_type=MESH,
        )
        for j in inner_order + [0] for k in order + [0] if j or k
    }

    slot_load.wait()
    slot = slot_ref[...]
    for k in order + [0]:
        wanted = slot - group_of[k] * capacity
        if capacity < lanes:
            wanted = jnp.where(wanted < capacity, wanted, -1)
        place[k] = one_hot(wanted, lanes)

    emb_load.wait()
    values = emb_ref[...].astype(jnp.float32)
    inverse = lax.rsqrt(jnp.sum(values * values, axis=1, keepdims=True) + 1e-06)
    unit = (values * inverse).astype(jnp.bfloat16)

    cid_load.wait()
    rank_load.wait()
    use_load.wait()
    cluster = cid_ref[...]
    rank = rank_ref[...]
    row = lax.broadcasted_iota(jnp.int32, (TAGS, rows), 0)
    tags = jnp.where(row == 0, jnp.bitwise_and(cluster, BASE - 1), 0)
    tags = jnp.where(row == 1, 1, tags)
    tags = jnp.where(row == 2, use_ref[...], tags)
    tags = jnp.where(row == 3, jnp.bitwise_and(rank, BASE - 1), tags)
    tags = jnp.where(row == 4, jnp.bitwise_and(jnp.right_shift(rank, 6), BASE - 1), tags)
    tags = jnp.where(row == 5, jnp.right_shift(rank, 12), tags)
    tags = tags.astype(jnp.float32).astype(jnp.bfloat16)

    for k in order + [0]:
        block = dot_nn(place[k], unit).astype(jnp.bfloat16)
        for h in range(halves):
            part = block[:, h * HALF:(h + 1) * HALF]
            if k:
                row_out[h, k] = part
            else:
                row_in[h, 0] = part
        block = dot_nt(tags, place[k]).astype(jnp.bfloat16)
        if k:
            tag_out[k] = block
        else:
            tag_in[0] = block

    pl.semaphore_wait(barrier, groups + inner - 2)
    for k in order:
        tag_copy[k].start()
    for k in order:
        row_copy[0, k].start()

    before = jnp.where(
        lax.broadcasted_iota(jnp.int32, (lanes, lanes), 0) < lax.broadcasted_iota(jnp.int32, (lanes, lanes), 1),
        1.0, 0.0,
    ).astype(jnp.bfloat16)
    bin_pad = round_up(inner, TAGS)
    seen = jnp.zeros((bin_pad, 1), jnp.float32)
    for k in order:
        tag_copy[k].wait_recv()
    for k in range(groups):
        arrived = tag_in[k].astype(jnp.float32)
        residue = jnp.bitwise_and(arrived[0:1].astype(jnp.int32), inner - 1)
        filled = arrived[1:2] > 0.5
        relative = jnp.full_like(residue, -1)
        for j in range(inner):
            relative = jnp.where(filled & (residue == inner_of[j]), j, relative)
        member = one_hot(relative, bin_pad)
        member_f = member.astype(jnp.float32)
        spot = dot_nn(member, before) + seen
        seen = seen + jnp.sum(member_f, axis=1, keepdims=True)
        spot = jnp.sum(member_f * spot, axis=0, keepdims=True).astype(jnp.int32)
        goal = jnp.where(filled, relative * bin_rows + spot, -1)
        pick[:, k * lanes:(k + 1) * lanes] = one_hot(goal, total)
    arrived_tags = jnp.concatenate([tag_in[k] for k in range(groups)], axis=1).astype(jnp.float32)
    row = lax.broadcasted_iota(jnp.int32, (TAGS, lanes), 0)
    lane = lax.broadcasted_iota(jnp.int32, (TAGS, lanes), 1)
    spots = [jnp.where(row == 6, lane, jnp.where(row == 7, k, 0)).astype(jnp.float32) for k in range(groups)]
    arrived_tags = (arrived_tags + jnp.concatenate(spots, axis=1)).astype(jnp.bfloat16)
    for k in inner_order + [0]:
        block = dot_nt(arrived_tags, pick[k * bin_rows:(k + 1) * bin_rows, :]).astype(jnp.bfloat16)
        if bin_rows < bin_lanes:
            block = jnp.concatenate([block, jnp.zeros((TAGS, bin_lanes - bin_rows), jnp.bfloat16)], axis=1)
        if k:
            tag2_out[k] = block
            tag2_copy[k].start()
        else:
            tag2_in[0] = block

    def forward(h):
        for k in order:
            row_copy[h, k].wait_recv()
        arrived_rows = row_in[h].reshape(groups * lanes, HALF)
        for k in inner_order + [0]:
            block = dot_nn(pick[k * bin_rows:(k + 1) * bin_rows, :], arrived_rows).astype(jnp.bfloat16)
            if k:
                row2_out[h, k] = block
                row2_copy[h, k].start()
            else:
                row2_in[h, 0] = block

    for h in range(halves - 1):
        for k in order:
            row_copy[h, k].wait_send()
        for k in order:
            row_copy[h + 1, k].start()
        forward(h)

    for k in inner_order:
        tag2_copy[k].wait_recv()
    same = lax.broadcasted_iota(jnp.int32, (bin_lanes, bin_lanes), 0) == lax.broadcasted_iota(
        jnp.int32, (bin_lanes, bin_lanes), 1
    )
    eye = jnp.where(same, 1.0, 0.0).astype(jnp.bfloat16)
    key_cluster, key_rank = [], []
    for k in range(inner):
        columns = dot_nt(eye, tag2_in[k])[:bin_rows]
        key_cluster.append(jnp.where(columns[:, 1:2] * columns[:, 2:3] > 0.5, columns[:, 0:1], -1.0))
        origin = jnp.where(columns[:, 1:2] > 0.5, columns[:, 6:7] + lanes * columns[:, 7:8], -1.0)
        lane = lax.broadcasted_iota(jnp.int32, (bin_rows, groups * lanes), 1).astype(jnp.float32)
        back_place[k] = jnp.where(lane == origin, 1.0, 0.0).astype(jnp.bfloat16)
        key_rank.append(columns[:, 3:4] + BASE * columns[:, 4:5] + (BASE * BASE) * columns[:, 5:6])
    for q in range(inner):
        lines = tag2_in[q].astype(jnp.float32)[:, :bin_rows]
        query_cluster = lines[0:1]
        query_rank = lines[3:4] + BASE * lines[4:5] + (BASE * BASE) * lines[5:6]
        for k in range(inner):
            matched = (key_cluster[k] == query_cluster) & (key_rank[k] < query_rank)
            limit[q, k * bin_rows:(k + 1) * bin_rows, :] = jnp.where(matched, 1e30, -1.0)

    forward(halves - 1)

    for h in range(halves):
        for k in inner_order:
            row2_copy[h, k].wait_recv()
    keys = jnp.concatenate([row2_in[h].reshape(total, HALF) for h in range(halves)], axis=1)
    for q in inner_order + [0]:
        queries = jnp.concatenate([row2_in[h, q] for h in range(halves)], axis=1)
        scores = jnp.minimum(dot_nt(keys, queries), limit[q])
        best = jnp.maximum(jnp.max(scores, axis=0, keepdims=True), -1.0)
        spread = join_rows(dot_nn(split_rows(best), back_place[q]))
        for k in order + [0]:
            block = spread[:, k * lanes:(k + 1) * lanes]
            if q or k:
                back_out[q, k] = block
                back_copy[q, k].start()
            else:
                back_in[0, 0] = block

    for copy in back_copy.values():
        copy.wait_recv()
    parts = []
    for k in range(groups):
        line = back_in[0, k]
        for j in range(1, inner):
            line = line + back_in[j, k]
        parts.append(split_rows(line))
    result = dot_nn(jnp.concatenate(parts, axis=1), place[...].reshape(groups * lanes, rows))
    out_ref[...] = join_rows(result)

    for k in order:
        row_copy[halves - 1, k].wait_send()
    for copies in (tag_copy, tag2_copy, row2_copy, back_copy):
        for copy in copies.values():
            copy.wait_send()


def local(embeddings, cluster_id, order_rank, send_slot, usable):
    groups, inner = lax.axis_size("group"), lax.axis_size("inner")
    rows, width = embeddings.shape
    capacity = 2 * rows // groups
    lanes = round_up(capacity, 128)
    bin_rows = 3 * rows // 2 // inner
    bin_lanes = round_up(bin_rows, 128)
    halves = width // HALF
    total = inner * bin_rows
    bf16, f32 = jnp.bfloat16, jnp.float32
    dma = pltpu.SemaphoreType.DMA
    sems = []
    for shape in ((groups,), (halves, groups), (inner,), (halves, inner), (inner, groups)):
        sems += [dma(shape), dma(shape)]
    out = pl.pallas_call(
        functools.partial(kernel, groups, inner, capacity, lanes, bin_rows, bin_lanes),
        out_shape=jax.ShapeDtypeStruct((1, rows), f32),
        in_specs=[pl.BlockSpec(memory_space=pltpu.HBM)] * 5,
        out_specs=pl.BlockSpec(memory_space=pltpu.VMEM),
        scratch_shapes=[
            pltpu.VMEM((rows, width), bf16),
            pltpu.VMEM((1, rows), jnp.int32),
            pltpu.VMEM((1, rows), jnp.int32),
            pltpu.VMEM((1, rows), jnp.int32),
            pltpu.VMEM((1, rows), jnp.int32),
            dma((5,)),
            pltpu.VMEM((groups, lanes, rows), bf16),
            pltpu.VMEM((total, groups * lanes), bf16),
            pltpu.VMEM((inner, total, bin_rows), f32),
            pltpu.VMEM((groups, TAGS, lanes), bf16),
            pltpu.VMEM((groups, TAGS, lanes), bf16),
            pltpu.VMEM((halves, groups, lanes, HALF), bf16),
            pltpu.VMEM((halves, groups, lanes, HALF), bf16),
            pltpu.VMEM((inner, TAGS, bin_lanes), bf16),
            pltpu.VMEM((inner, TAGS, bin_lanes), bf16),
            pltpu.VMEM((halves, inner, bin_rows, HALF), bf16),
            pltpu.VMEM((halves, inner, bin_rows, HALF), bf16),
            pltpu.VMEM((inner, bin_rows, groups * lanes), bf16),
            pltpu.VMEM((inner, groups, 1, lanes), f32),
            pltpu.VMEM((inner, groups, 1, lanes), f32),
        ] + sems,
        compiler_params=pltpu.CompilerParams(
            collective_id=0, has_side_effects=True, vmem_limit_bytes=40 * 1024 * 1024
        ),
        name="dedup",
    )(
        embeddings,
        cluster_id.reshape(1, rows),
        order_rank.reshape(1, rows),
        send_slot.reshape(1, rows),
        usable.reshape(1, rows),
    )
    return out.reshape(rows)


def solution(mesh):
    placed = (
        P(("group", "inner"), None),
        P(("group", "inner")),
        P(("group", "inner")),
        P(("group", "inner")),
        P(("group", "inner")),
    )
    return jax.shard_map(
        local, mesh=mesh, in_specs=placed, out_specs=P(("group", "inner")), check_vma=False
    )
```

```python
import functools

import jax
import jax.numpy as jnp
from jax import lax
from jax.experimental import pallas as pl
from jax.experimental.pallas import tpu as pltpu
from jax.sharding import PartitionSpec as P

MESH = pl.DeviceIdType.MESH
BASE = 64
HALF = 128
TAGS = 16


def round_up(value, step):
    return (value + step - 1) // step * step


def partner(me, k):
    result, bit = me, 1
    while bit <= k:
        if k & bit:
            result = result + bit * (1 - 2 * lax.rem(lax.div(me, bit), 2))
        bit *= 2
    return result


def split_rows(value):
    high = value.astype(jnp.bfloat16).astype(jnp.float32)
    rest = value - high
    mid = rest.astype(jnp.bfloat16).astype(jnp.float32)
    low = rest - mid
    row = lax.broadcasted_iota(jnp.int32, (TAGS, value.shape[1]), 0)
    parts = jnp.where(row == 0, high, jnp.where(row == 1, mid, jnp.where(row == 2, low, 0.0)))
    return parts.astype(jnp.bfloat16)


def join_rows(parts):
    return (parts[0:1] + parts[1:2]) + parts[2:3]


def one_hot(position, rows):
    row = lax.broadcasted_iota(jnp.int32, (rows, position.shape[1]), 0)
    return jnp.where(row == position, 1.0, 0.0).astype(jnp.bfloat16)


def dot_nt(a, b):
    return lax.dot_general(a, b, (((1,), (1,)), ((), ())), preferred_element_type=jnp.float32)


def dot_nn(a, b):
    return jnp.dot(a, b, preferred_element_type=jnp.float32)


def kernel(
    groups, inner, capacity, lanes, bin_rows, bin_lanes,
    emb_hbm, cid_hbm, rank_hbm, slot_hbm, use_hbm, out_ref,
    emb_ref, cid_ref, rank_ref, slot_ref, use_ref, load,
    place, pick, limit,
    tag_out, tag_in, row_out, row_in, tag2_out, tag2_in, row2_out, row2_in,
    back_place, back_out, back_in,
    tag_s, tag_r, row_s, row_r, tag2_s, tag2_r, row2_s, row2_r, back_s, back_r,
):
    rows, width = emb_ref.shape
    halves = width // HALF
    total = inner * bin_rows
    my_group, my_inner = lax.axis_index("group"), lax.axis_index("inner")
    group_of = [partner(my_group, k) for k in range(groups)]
    inner_of = [partner(my_inner, k) for k in range(inner)]

    order = list(range(groups - 2, 0, -2))
    order = [k for pair in order for k in (pair, pair + 1)] + [1]
    inner_order = list(range(inner - 1, 0, -1))
    barrier = pltpu.get_barrier_semaphore()
    for k in order:
        pl.semaphore_signal(barrier, inc=1, device_id={"group": group_of[k]}, device_id_type=MESH)
    for k in inner_order:
        pl.semaphore_signal(barrier, inc=1, device_id={"inner": inner_of[k]}, device_id_type=MESH)

    slot_load, emb_load, cid_load, rank_load, use_load = [
        pltpu.make_async_copy(src, dst, load.at[n])
        for n, (src, dst) in enumerate(
            ((slot_hbm, slot_ref), (emb_hbm, emb_ref), (cid_hbm, cid_ref), (rank_hbm, rank_ref), (use_hbm, use_ref))
        )
    ]
    for copy in (slot_load, emb_load, cid_load, rank_load, use_load):
        copy.start()


    def remote(src, dst, send, recv, axis, peer):
        return pltpu.make_async_remote_copy(
            src_ref=src, dst_ref=dst, send_sem=send, recv_sem=recv,
            device_id={axis: peer}, device_id_type=MESH,
        )

    tag_copy = {k: remote(tag_out.at[k], tag_in.at[k], tag_s.at[k], tag_r.at[k], "group", group_of[k]) for k in order}
    row_copy = {
        (h, k): remote(row_out.at[h, k], row_in.at[h, k], row_s.at[h, k], row_r.at[h, k], "group", group_of[k])
        for h in range(halves) for k in order
    }
    tag2_copy = {k: remote(tag2_out.at[k], tag2_in.at[k], tag2_s.at[k], tag2_r.at[k], "inner", inner_of[k]) for k in inner_order}
    row2_copy = {
        (h, k): remote(row2_out.at[h, k], row2_in.at[h, k], row2_s.at[h, k], row2_r.at[h, k], "inner", inner_of[k])
        for h in range(halves) for k in inner_order
    }
    back_copy = {
        (j, k): pltpu.make_async_remote_copy(
            src_ref=back_out.at[j, k], dst_ref=back_in.at[j, k], send_sem=back_s.at[j, k], recv_sem=back_r.at[j, k],
            device_id=(group_of[k], inner_of[j]), device_id_type=MESH,
        )
        for j in inner_order + [0] for k in order + [0] if j or k
    }

    slot_load.wait()
    slot = slot_ref[...]
    for k in order + [0]:
        wanted = slot - group_of[k] * capacity
        if capacity < lanes:
            wanted = jnp.where(wanted < capacity, wanted, -1)
        place[k] = one_hot(wanted, lanes)

    emb_load.wait()
    values = emb_ref[...].astype(jnp.float32)
    inverse = lax.rsqrt(jnp.sum(values * values, axis=1, keepdims=True) + 1e-06)
    unit = (values * inverse).astype(jnp.bfloat16)

    cid_load.wait()
    rank_load.wait()
    use_load.wait()
    cluster = cid_ref[...]
    rank = rank_ref[...]
    row = lax.broadcasted_iota(jnp.int32, (TAGS, rows), 0)
    tags = jnp.where(row == 0, jnp.bitwise_and(cluster, BASE - 1), 0)
    tags = jnp.where(row == 1, 1, tags)
    tags = jnp.where(row == 2, use_ref[...], tags)
    tags = jnp.where(row == 3, jnp.bitwise_and(rank, BASE - 1), tags)
    tags = jnp.where(row == 4, jnp.bitwise_and(jnp.right_shift(rank, 6), BASE - 1), tags)
    tags = jnp.where(row == 5, jnp.right_shift(rank, 12), tags)
    tags = tags.astype(jnp.float32).astype(jnp.bfloat16)

    for k in order + [0]:
        block = dot_nn(place[k], unit).astype(jnp.bfloat16)
        for h in range(halves):
            part = block[:, h * HALF:(h + 1) * HALF]
            if k:
                row_out[h, k] = part
            else:
                row_in[h, 0] = part
        block = dot_nt(tags, place[k])
        lines = (block[0:1] + block[1:2], block[2:3], block[3:4] + BASE * block[4:5] + (BASE * BASE) * block[5:6])
        for n, line in enumerate(lines):
            if k:
                tag_out[k, n] = line
            else:
                tag_in[0, n] = line

    pl.semaphore_wait(barrier, groups + inner - 2)
    for k in order:
        tag_copy[k].start()
    for k in order:
        row_copy[0, k].start()

    before = jnp.where(
        lax.broadcasted_iota(jnp.int32, (lanes, lanes), 0) < lax.broadcasted_iota(jnp.int32, (lanes, lanes), 1),
        1.0, 0.0,
    ).astype(jnp.bfloat16)
    bin_pad = round_up(inner, TAGS)
    seen = jnp.zeros((bin_pad, 1), jnp.float32)
    arrived_tags = []
    for k in order:
        tag_copy[k].wait_recv()
    for k in range(groups):
        arrived = tag_in[k, 0].astype(jnp.int32)
        filled = arrived > 0
        member_of = jnp.where(filled, arrived - 1, 0)
        residue = jnp.bitwise_and(member_of, inner - 1)
        relative = jnp.full_like(residue, -1)
        for j in range(inner):
            relative = jnp.where(filled & (residue == inner_of[j]), j, relative)
        member = one_hot(relative, bin_pad)
        member_f = member.astype(jnp.float32)
        spot = dot_nn(member, before) + seen
        seen = seen + jnp.sum(member_f, axis=1, keepdims=True)
        spot = jnp.sum(member_f * spot, axis=0, keepdims=True).astype(jnp.int32)
        goal = jnp.where(filled, relative * bin_rows + spot, -1)
        pick[:, k * lanes:(k + 1) * lanes] = one_hot(goal, total)
        rank = tag_in[k, 2].astype(jnp.int32)
        row = lax.broadcasted_iota(jnp.int32, (TAGS, lanes), 0)
        lane = lax.broadcasted_iota(jnp.int32, (TAGS, lanes), 1)
        lines = jnp.where(row == 0, member_of, 0)
        lines = jnp.where((row == 1) & filled, 1, lines)
        lines = jnp.where(row == 2, tag_in[k, 1].astype(jnp.int32), lines)
        lines = jnp.where(row == 3, jnp.bitwise_and(rank, BASE - 1), lines)
        lines = jnp.where(row == 4, jnp.bitwise_and(jnp.right_shift(rank, 6), BASE - 1), lines)
        lines = jnp.where(row == 5, jnp.right_shift(rank, 12), lines)
        lines = jnp.where(row == 6, lane, lines)
        lines = jnp.where(row == 7, k, lines)
        arrived_tags.append(lines.astype(jnp.float32).astype(jnp.bfloat16))
    arrived_tags = jnp.concatenate(arrived_tags, axis=1)
    for k in inner_order + [0]:
        block = dot_nt(arrived_tags, pick[k * bin_rows:(k + 1) * bin_rows, :]).astype(jnp.bfloat16)
        if bin_rows < bin_lanes:
            block = jnp.concatenate([block, jnp.zeros((TAGS, bin_lanes - bin_rows), jnp.bfloat16)], axis=1)
        if k:
            tag2_out[k] = block
            tag2_copy[k].start()
        else:
            tag2_in[0] = block

    def forward(h):
        for k in order:
            row_copy[h, k].wait_recv()
        arrived_rows = row_in[h].reshape(groups * lanes, HALF)
        for k in inner_order + [0]:
            block = dot_nn(pick[k * bin_rows:(k + 1) * bin_rows, :], arrived_rows).astype(jnp.bfloat16)
            if k:
                row2_out[h, k] = block
                row2_copy[h, k].start()
            else:
                row2_in[h, 0] = block

    for h in range(halves - 1):
        for k in order:
            row_copy[h, k].wait_send()
        for k in order:
            row_copy[h + 1, k].start()
        forward(h)

    for k in inner_order:
        tag2_copy[k].wait_recv()
    same = lax.broadcasted_iota(jnp.int32, (bin_lanes, bin_lanes), 0) == lax.broadcasted_iota(
        jnp.int32, (bin_lanes, bin_lanes), 1
    )
    eye = jnp.where(same, 1.0, 0.0).astype(jnp.bfloat16)
    key_cluster, key_rank = [], []
    for k in range(inner):
        columns = dot_nt(eye, tag2_in[k])[:bin_rows]
        key_cluster.append(jnp.where(columns[:, 1:2] * columns[:, 2:3] > 0.5, columns[:, 0:1], -1.0))
        origin = jnp.where(columns[:, 1:2] > 0.5, columns[:, 6:7] + lanes * columns[:, 7:8], -1.0)
        lane = lax.broadcasted_iota(jnp.int32, (bin_rows, groups * lanes), 1).astype(jnp.float32)
        back_place[k] = jnp.where(lane == origin, 1.0, 0.0).astype(jnp.bfloat16)
        key_rank.append(columns[:, 3:4] + BASE * columns[:, 4:5] + (BASE * BASE) * columns[:, 5:6])
    for q in range(inner):
        lines = tag2_in[q].astype(jnp.float32)[:, :bin_rows]
        query_cluster = lines[0:1]
        query_rank = lines[3:4] + BASE * lines[4:5] + (BASE * BASE) * lines[5:6]
        for k in range(inner):
            matched = (key_cluster[k] == query_cluster) & (key_rank[k] < query_rank)
            limit[q, k * bin_rows:(k + 1) * bin_rows, :] = jnp.where(matched, 1e30, -1.0)

    forward(halves - 1)

    for h in range(halves):
        for k in inner_order:
            row2_copy[h, k].wait_recv()
    keys = jnp.concatenate([row2_in[h].reshape(total, HALF) for h in range(halves)], axis=1)
    for q in inner_order + [0]:
        queries = jnp.concatenate([row2_in[h, q] for h in range(halves)], axis=1)
        scores = jnp.minimum(dot_nt(keys, queries), limit[q])
        best = jnp.maximum(jnp.max(scores, axis=0, keepdims=True), -1.0)
        spread = join_rows(dot_nn(split_rows(best), back_place[q]))
        for k in order + [0]:
            block = spread[:, k * lanes:(k + 1) * lanes]
            if q or k:
                back_out[q, k] = block
                back_copy[q, k].start()
            else:
                back_in[0, 0] = block

    for copy in back_copy.values():
        copy.wait_recv()
    parts = []
    for k in range(groups):
        line = back_in[0, k]
        for j in range(1, inner):
            line = line + back_in[j, k]
        parts.append(split_rows(line))
    result = dot_nn(jnp.concatenate(parts, axis=1), place[...].reshape(groups * lanes, rows))
    out_ref[...] = join_rows(result)

    for k in order:
        row_copy[halves - 1, k].wait_send()
    for copies in (tag_copy, tag2_copy, row2_copy, back_copy):
        for copy in copies.values():
            copy.wait_send()


def local(embeddings, cluster_id, order_rank, send_slot, usable):
    groups, inner = lax.axis_size("group"), lax.axis_size("inner")
    rows, width = embeddings.shape
    capacity = 2 * rows // groups
    lanes = round_up(capacity, 128)
    bin_rows = 3 * rows // 2 // inner
    bin_lanes = round_up(bin_rows, 128)
    halves = width // HALF
    total = inner * bin_rows
    bf16, f32 = jnp.bfloat16, jnp.float32
    dma = pltpu.SemaphoreType.DMA
    sems = []
    for shape in ((groups,), (halves, groups), (inner,), (halves, inner), (inner, groups)):
        sems += [dma(shape), dma(shape)]
    out = pl.pallas_call(
        functools.partial(kernel, groups, inner, capacity, lanes, bin_rows, bin_lanes),
        out_shape=jax.ShapeDtypeStruct((1, rows), f32),
        in_specs=[pl.BlockSpec(memory_space=pltpu.HBM)] * 5,
        out_specs=pl.BlockSpec(memory_space=pltpu.VMEM),
        scratch_shapes=[
            pltpu.VMEM((rows, width), bf16),
            pltpu.VMEM((1, rows), jnp.int32),
            pltpu.VMEM((1, rows), jnp.int32),
            pltpu.VMEM((1, rows), jnp.int32),
            pltpu.VMEM((1, rows), jnp.int32),
            dma((5,)),
            pltpu.VMEM((groups, lanes, rows), bf16),
            pltpu.VMEM((total, groups * lanes), bf16),
            pltpu.VMEM((inner, total, bin_rows), f32),
            pltpu.VMEM((groups, 3, 1, lanes), f32),
            pltpu.VMEM((groups, 3, 1, lanes), f32),
            pltpu.VMEM((halves, groups, lanes, HALF), bf16),
            pltpu.VMEM((halves, groups, lanes, HALF), bf16),
            pltpu.VMEM((inner, TAGS, bin_lanes), bf16),
            pltpu.VMEM((inner, TAGS, bin_lanes), bf16),
            pltpu.VMEM((halves, inner, bin_rows, HALF), bf16),
            pltpu.VMEM((halves, inner, bin_rows, HALF), bf16),
            pltpu.VMEM((inner, bin_rows, groups * lanes), bf16),
            pltpu.VMEM((inner, groups, 1, lanes), f32),
            pltpu.VMEM((inner, groups, 1, lanes), f32),
        ] + sems,
        compiler_params=pltpu.CompilerParams(
            collective_id=0, has_side_effects=True, vmem_limit_bytes=40 * 1024 * 1024
        ),
        name="dedup",
    )(
        embeddings,
        cluster_id.reshape(1, rows),
        order_rank.reshape(1, rows),
        send_slot.reshape(1, rows),
        usable.reshape(1, rows),
    )
    return out.reshape(rows)


def solution(mesh):
    placed = (
        P(("group", "inner"), None),
        P(("group", "inner")),
        P(("group", "inner")),
        P(("group", "inner")),
        P(("group", "inner")),
    )
    return jax.shard_map(
        local, mesh=mesh, in_specs=placed, out_specs=P(("group", "inner")), check_vma=False
    )
```

```python
import functools

import jax
import jax.numpy as jnp
from jax import lax
from jax.experimental import pallas as pl
from jax.experimental.pallas import tpu as pltpu
from jax.sharding import PartitionSpec as P

MESH = pl.DeviceIdType.MESH
BASE = 64
HALF = 128
TAGS = 16


def round_up(value, step):
    return (value + step - 1) // step * step


def partner(me, k):
    result, bit = me, 1
    while bit <= k:
        if k & bit:
            result = result + bit * (1 - 2 * lax.rem(lax.div(me, bit), 2))
        bit *= 2
    return result


def split_rows(value):
    high = value.astype(jnp.bfloat16).astype(jnp.float32)
    rest = value - high
    mid = rest.astype(jnp.bfloat16).astype(jnp.float32)
    low = rest - mid
    row = lax.broadcasted_iota(jnp.int32, (TAGS, value.shape[1]), 0)
    parts = jnp.where(row == 0, high, jnp.where(row == 1, mid, jnp.where(row == 2, low, 0.0)))
    return parts.astype(jnp.bfloat16)


def join_rows(parts):
    return (parts[0:1] + parts[1:2]) + parts[2:3]


def one_hot(position, rows):
    row = lax.broadcasted_iota(jnp.int32, (rows, position.shape[1]), 0)
    return jnp.where(row == position, 1.0, 0.0).astype(jnp.bfloat16)


def dot_nt(a, b):
    return lax.dot_general(a, b, (((1,), (1,)), ((), ())), preferred_element_type=jnp.float32)


def dot_nn(a, b):
    return jnp.dot(a, b, preferred_element_type=jnp.float32)


def kernel(
    groups, inner, capacity, lanes, bin_rows, bin_lanes,
    emb_hbm, cid_hbm, rank_hbm, slot_hbm, use_hbm, out_ref,
    emb_ref, cid_ref, rank_ref, slot_ref, use_ref, load,
    place, pick, limit,
    tag_out, tag_in, row_out, row_in, tag2_out, tag2_in, row2_out, row2_in,
    back_place, back_out, back_in,
    tag_s, tag_r, row_s, row_r, tag2_s, tag2_r, row2_s, row2_r, back_s, back_r,
):
    rows, width = emb_ref.shape
    halves = width // HALF
    total = inner * bin_rows
    my_group, my_inner = lax.axis_index("group"), lax.axis_index("inner")
    group_of = [partner(my_group, k) for k in range(groups)]
    inner_of = [partner(my_inner, k) for k in range(inner)]

    order = list(range(groups - 2, 0, -2))
    order = [k for pair in order for k in (pair, pair + 1)] + [1]
    inner_order = list(range(inner - 1, 0, -1))
    barrier = pltpu.get_barrier_semaphore()
    for k in order:
        pl.semaphore_signal(barrier, inc=1, device_id={"group": group_of[k]}, device_id_type=MESH)
    for k in inner_order:
        pl.semaphore_signal(barrier, inc=1, device_id={"inner": inner_of[k]}, device_id_type=MESH)

    slot_load, emb_load, cid_load, rank_load, use_load = [
        pltpu.make_async_copy(src, dst, load.at[n])
        for n, (src, dst) in enumerate(
            ((slot_hbm, slot_ref), (emb_hbm, emb_ref), (cid_hbm, cid_ref), (rank_hbm, rank_ref), (use_hbm, use_ref))
        )
    ]
    for copy in (slot_load, emb_load, cid_load, rank_load, use_load):
        copy.start()


    def remote(src, dst, send, recv, axis, peer):
        return pltpu.make_async_remote_copy(
            src_ref=src, dst_ref=dst, send_sem=send, recv_sem=recv,
            device_id={axis: peer}, device_id_type=MESH,
        )

    tag_copy = {k: remote(tag_out.at[k], tag_in.at[k], tag_s.at[k], tag_r.at[k], "group", group_of[k]) for k in order}
    row_copy = {
        (h, k): remote(row_out.at[h, k], row_in.at[h, k], row_s.at[h, k], row_r.at[h, k], "group", group_of[k])
        for h in range(halves) for k in order
    }
    tag2_copy = {k: remote(tag2_out.at[k], tag2_in.at[k], tag2_s.at[k], tag2_r.at[k], "inner", inner_of[k]) for k in inner_order}
    row2_copy = {
        (h, k): remote(row2_out.at[h, k], row2_in.at[h, k], row2_s.at[h, k], row2_r.at[h, k], "inner", inner_of[k])
        for h in range(halves) for k in inner_order
    }
    back_copy = {
        (j, k): pltpu.make_async_remote_copy(
            src_ref=back_out.at[j, k], dst_ref=back_in.at[j, k], send_sem=back_s.at[j, k], recv_sem=back_r.at[j, k],
            device_id=(group_of[k], inner_of[j]), device_id_type=MESH,
        )
        for j in inner_order + [0] for k in order + [0] if j or k
    }

    slot_load.wait()
    slot = slot_ref[...]
    for k in order + [0]:
        wanted = slot - group_of[k] * capacity
        if capacity < lanes:
            wanted = jnp.where(wanted < capacity, wanted, -1)
        place[k] = one_hot(wanted, lanes)

    emb_load.wait()
    values = emb_ref[...].astype(jnp.float32)
    inverse = lax.rsqrt(jnp.sum(values * values, axis=1, keepdims=True) + 1e-06)
    unit = (values * inverse).astype(jnp.bfloat16)

    cid_load.wait()
    rank_load.wait()
    use_load.wait()
    cluster = cid_ref[...]
    rank = rank_ref[...]
    row = lax.broadcasted_iota(jnp.int32, (TAGS, rows), 0)
    tags = jnp.where(row == 0, jnp.bitwise_and(cluster, BASE - 1), 0)
    tags = jnp.where(row == 1, 1, tags)
    tags = jnp.where(row == 2, use_ref[...], tags)
    tags = jnp.where(row == 3, jnp.bitwise_and(rank, BASE - 1), tags)
    tags = jnp.where(row == 4, jnp.bitwise_and(jnp.right_shift(rank, 6), BASE - 1), tags)
    tags = jnp.where(row == 5, jnp.right_shift(rank, 12), tags)
    tags = tags.astype(jnp.float32).astype(jnp.bfloat16)

    for k in order + [0]:
        block = dot_nn(place[k], unit).astype(jnp.bfloat16)
        for h in range(halves):
            part = block[:, h * HALF:(h + 1) * HALF]
            if k:
                row_out[h, k] = part
            else:
                row_in[h, 0] = part
        block = dot_nt(tags, place[k])
        lines = (block[0:1] + block[1:2], block[2:3], block[3:4] + BASE * block[4:5] + (BASE * BASE) * block[5:6])
        for n, line in enumerate(lines):
            if k:
                tag_out[k, n] = line
            else:
                tag_in[0, n] = line

    pl.semaphore_wait(barrier, groups + inner - 2)
    for k in order:
        tag_copy[k].start()
    for k in order:
        row_copy[0, k].start()

    before = jnp.where(
        lax.broadcasted_iota(jnp.int32, (lanes, lanes), 0) < lax.broadcasted_iota(jnp.int32, (lanes, lanes), 1),
        1.0, 0.0,
    ).astype(jnp.bfloat16)
    bin_pad = round_up(inner, TAGS)
    seen = jnp.zeros((bin_pad, 1), jnp.float32)
    arrived_tags = []
    for k in order:
        tag_copy[k].wait_recv()
    for k in range(groups):
        arrived = tag_in[k, 0].astype(jnp.int32)
        filled = arrived > 0
        member_of = jnp.where(filled, arrived - 1, 0)
        residue = jnp.bitwise_and(member_of, inner - 1)
        relative = jnp.full_like(residue, -1)
        for j in range(inner):
            relative = jnp.where(filled & (residue == inner_of[j]), j, relative)
        member = one_hot(relative, bin_pad)
        member_f = member.astype(jnp.float32)
        spot = dot_nn(member, before) + seen
        seen = seen + jnp.sum(member_f, axis=1, keepdims=True)
        spot = jnp.sum(member_f * spot, axis=0, keepdims=True).astype(jnp.int32)
        goal = jnp.where(filled, relative * bin_rows + spot, -1)
        pick[:, k * lanes:(k + 1) * lanes] = one_hot(goal, total)
        rank = tag_in[k, 2].astype(jnp.int32)
        row = lax.broadcasted_iota(jnp.int32, (TAGS, lanes), 0)
        lane = lax.broadcasted_iota(jnp.int32, (TAGS, lanes), 1)
        lines = jnp.where(row == 0, member_of, 0)
        lines = jnp.where((row == 1) & filled, 1, lines)
        lines = jnp.where(row == 2, tag_in[k, 1].astype(jnp.int32), lines)
        lines = jnp.where(row == 3, jnp.bitwise_and(rank, BASE - 1), lines)
        lines = jnp.where(row == 4, jnp.bitwise_and(jnp.right_shift(rank, 6), BASE - 1), lines)
        lines = jnp.where(row == 5, jnp.right_shift(rank, 12), lines)
        lines = jnp.where(row == 6, lane, lines)
        lines = jnp.where(row == 7, k, lines)
        arrived_tags.append(lines.astype(jnp.float32).astype(jnp.bfloat16))
    arrived_tags = jnp.concatenate(arrived_tags, axis=1)
    for k in inner_order + [0]:
        block = dot_nt(arrived_tags, pick[k * bin_rows:(k + 1) * bin_rows, :]).astype(jnp.bfloat16)
        if bin_rows < bin_lanes:
            block = jnp.concatenate([block, jnp.zeros((TAGS, bin_lanes - bin_rows), jnp.bfloat16)], axis=1)
        if k:
            tag2_out[k] = block
            tag2_copy[k].start()
        else:
            tag2_in[0] = block

    def forward(h):
        for k in order:
            row_copy[h, k].wait_recv()
        arrived_rows = row_in[h].reshape(groups * lanes, HALF)
        for k in inner_order + [0]:
            block = dot_nn(pick[k * bin_rows:(k + 1) * bin_rows, :], arrived_rows).astype(jnp.bfloat16)
            if k:
                row2_out[h, k] = block
                row2_copy[h, k].start()
            else:
                row2_in[h, 0] = block

    for h in range(halves - 1):
        for k in order:
            row_copy[h, k].wait_send()
        for k in order:
            row_copy[h + 1, k].start()
        forward(h)

    for k in inner_order:
        tag2_copy[k].wait_recv()
    same = lax.broadcasted_iota(jnp.int32, (bin_lanes, bin_lanes), 0) == lax.broadcasted_iota(
        jnp.int32, (bin_lanes, bin_lanes), 1
    )
    eye = jnp.where(same, 1.0, 0.0).astype(jnp.bfloat16)
    key_cluster, key_rank = [], []
    for k in range(inner):
        columns = dot_nt(eye, tag2_in[k])[:bin_rows]
        key_cluster.append(jnp.where(columns[:, 1:2] * columns[:, 2:3] > 0.5, columns[:, 0:1], -1.0))
        origin = jnp.where(columns[:, 1:2] > 0.5, columns[:, 6:7] + lanes * columns[:, 7:8], -1.0)
        lane = lax.broadcasted_iota(jnp.int32, (bin_rows, groups * lanes), 1).astype(jnp.float32)
        back_place[k] = jnp.where(lane == origin, 1.0, 0.0).astype(jnp.bfloat16)
        key_rank.append(columns[:, 3:4] + BASE * columns[:, 4:5] + (BASE * BASE) * columns[:, 5:6])
    for q in range(inner):
        lines = tag2_in[q].astype(jnp.float32)[:, :bin_rows]
        query_cluster = lines[0:1]
        query_rank = lines[3:4] + BASE * lines[4:5] + (BASE * BASE) * lines[5:6]
        for k in range(inner):
            matched = (key_cluster[k] == query_cluster) & (key_rank[k] < query_rank)
            limit[q, k * bin_rows:(k + 1) * bin_rows, :] = jnp.where(matched, 1e30, -1.0)

    forward(halves - 1)

    for h in range(halves):
        for k in inner_order:
            row2_copy[h, k].wait_recv()
    keys = jnp.concatenate([row2_in[h].reshape(total, HALF) for h in range(halves)], axis=1)
    bests = {}
    for q in inner_order + [0]:
        queries = jnp.concatenate([row2_in[h, q] for h in range(halves)], axis=1)
        scores = jnp.minimum(dot_nt(keys, queries), limit[q])
        best = jnp.maximum(jnp.max(scores, axis=0, keepdims=True), -1.0)
        bests[q] = best
    for q in inner_order + [0]:
        spread = join_rows(dot_nn(split_rows(bests[q]), back_place[q]))
        for k in order + [0]:
            block = spread[:, k * lanes:(k + 1) * lanes]
            if q or k:
                back_out[q, k] = block
                back_copy[q, k].start()
            else:
                back_in[0, 0] = block

    for copy in back_copy.values():
        copy.wait_recv()
    parts = []
    for k in range(groups):
        line = back_in[0, k]
        for j in range(1, inner):
            line = line + back_in[j, k]
        parts.append(split_rows(line))
    result = dot_nn(jnp.concatenate(parts, axis=1), place[...].reshape(groups * lanes, rows))
    out_ref[...] = join_rows(result)

    for k in order:
        row_copy[halves - 1, k].wait_send()
    for copies in (tag_copy, tag2_copy, row2_copy, back_copy):
        for copy in copies.values():
            copy.wait_send()


def local(embeddings, cluster_id, order_rank, send_slot, usable):
    groups, inner = lax.axis_size("group"), lax.axis_size("inner")
    rows, width = embeddings.shape
    capacity = 2 * rows // groups
    lanes = round_up(capacity, 128)
    bin_rows = 3 * rows // 2 // inner
    bin_lanes = round_up(bin_rows, 128)
    halves = width // HALF
    total = inner * bin_rows
    bf16, f32 = jnp.bfloat16, jnp.float32
    dma = pltpu.SemaphoreType.DMA
    sems = []
    for shape in ((groups,), (halves, groups), (inner,), (halves, inner), (inner, groups)):
        sems += [dma(shape), dma(shape)]
    out = pl.pallas_call(
        functools.partial(kernel, groups, inner, capacity, lanes, bin_rows, bin_lanes),
        out_shape=jax.ShapeDtypeStruct((1, rows), f32),
        in_specs=[pl.BlockSpec(memory_space=pltpu.HBM)] * 5,
        out_specs=pl.BlockSpec(memory_space=pltpu.VMEM),
        scratch_shapes=[
            pltpu.VMEM((rows, width), bf16),
            pltpu.VMEM((1, rows), jnp.int32),
            pltpu.VMEM((1, rows), jnp.int32),
            pltpu.VMEM((1, rows), jnp.int32),
            pltpu.VMEM((1, rows), jnp.int32),
            dma((5,)),
            pltpu.VMEM((groups, lanes, rows), bf16),
            pltpu.VMEM((total, groups * lanes), bf16),
            pltpu.VMEM((inner, total, bin_rows), f32),
            pltpu.VMEM((groups, 3, 1, lanes), f32),
            pltpu.VMEM((groups, 3, 1, lanes), f32),
            pltpu.VMEM((halves, groups, lanes, HALF), bf16),
            pltpu.VMEM((halves, groups, lanes, HALF), bf16),
            pltpu.VMEM((inner, TAGS, bin_lanes), bf16),
            pltpu.VMEM((inner, TAGS, bin_lanes), bf16),
            pltpu.VMEM((halves, inner, bin_rows, HALF), bf16),
            pltpu.VMEM((halves, inner, bin_rows, HALF), bf16),
            pltpu.VMEM((inner, bin_rows, groups * lanes), bf16),
            pltpu.VMEM((inner, groups, 1, lanes), f32),
            pltpu.VMEM((inner, groups, 1, lanes), f32),
        ] + sems,
        compiler_params=pltpu.CompilerParams(
            collective_id=0, has_side_effects=True, vmem_limit_bytes=40 * 1024 * 1024
        ),
        name="dedup",
    )(
        embeddings,
        cluster_id.reshape(1, rows),
        order_rank.reshape(1, rows),
        send_slot.reshape(1, rows),
        usable.reshape(1, rows),
    )
    return out.reshape(rows)


def solution(mesh):
    placed = (
        P(("group", "inner"), None),
        P(("group", "inner")),
        P(("group", "inner")),
        P(("group", "inner")),
        P(("group", "inner")),
    )
    return jax.shard_map(
        local, mesh=mesh, in_specs=placed, out_specs=P(("group", "inner")), check_vma=False
    )
```
